32 devices in a mesh: parts: 1, row: 8 (over z, y), col: 1, depth: 4 (over x, core).
Axes of the slice: x: 2, y: 2, z: 4, core: 2. Of those that a mesh axis runs over, the one named last changes fastest.
Arguments:
- activations: bfloat16 [4, 256, 8192], P(('parts', 'depth'), 'row', 'col'), may hold values from -6 to 6
- hidden_grads: bfloat16 [4, 256, 16384], P(('parts', 'depth'), 'col', 'row'), may hold values from -0.1875 to 0.1875
Outputs:
- weight_grad: bfloat16 [8192, 16384], P(('parts', 'col', 'depth'), 'row')
The draws below stay inside these ranges and needn't reach their ends.
All inputs are finite; a program needn't handle non-finite values.
Results may differ from the reference program's by a relative error of at most 0.013.
Values may be sent and summed in bfloat16 or wider, within the bound.
A program may use at most 128 MiB of HBM per device.

```python
import jax
import jax.numpy as jnp
from jax import lax

D = 8192
FF = 16384
MICRO = 4
MB_TOK = 256
TOKENS = 1024


def block_scale(key, extent, cuts, least, high):
    loudness, own = 1.0, jax.random.fold_in(key, 6)
    for dim, parts in cuts:
        draws = jnp.exp(jax.random.uniform(jax.random.fold_in(own, dim), (parts,), jnp.float32, least / len(cuts), high / len(cuts)))
        loudness = loudness * jnp.repeat(draws, extent[dim] // parts).reshape([-1 if axis == dim else 1 for axis in range(len(extent))])
    return loudness


def scatter_about(own_key, shape, width, bound, shards=(), held_as=jnp.bfloat16):
    drawn = jax.random.normal(own_key, shape, jnp.float32) * width
    if len(shards) > 0:
        drawn = block_scale(own_key, shape, shards, -0.22, 0.18) * drawn
    return jnp.clip(drawn, min=-bound, max=bound).astype(held_as)


def setup_inputs(seed: int = 0, part: int = 0) -> dict:
    streams_of = jax.random.split(jax.random.key(seed), 3)
    part_keys = jax.random.split(jax.random.fold_in(streams_of[2], part), 3)
    return {
        "activations": scatter_about(part_keys[0], (MICRO, MB_TOK, D), 1.0, 6.0, ((0, 4), (1, 8))),
        "hidden_grads": scatter_about(part_keys[1], (MICRO, MB_TOK, FF), TOKENS ** -0.5, 0.1875, ((0, 4), (2, 8))),
    }


def reference(activations, hidden_grads):
    def accumulate(running, inputs_pair):
        block_acts, block_grads = inputs_pair
        partial_value = jnp.dot(block_acts.T, block_grads, preferred_element_type=jnp.float32)
        partial_value = lax.optimization_barrier(partial_value.astype(jnp.bfloat16)).astype(jnp.float32)
        return running + partial_value, None

    running, _ = lax.scan(accumulate, jnp.zeros((D, FF), jnp.float32), (activations, hidden_grads))
    return running.astype(jnp.bfloat16)
```

```python
import jax
import jax.numpy as jnp
from jax import lax
from jax.sharding import PartitionSpec as P


def local(activations, hidden_grads):
    swapped = lax.all_to_all(activations, "depth", split_axis=2, concat_axis=0, tiled=True)
    acts = lax.all_gather(swapped, "row", axis=1, tiled=True)
    grads = lax.all_gather(hidden_grads, "depth", axis=0, tiled=True)
    grads = lax.all_gather(grads, "col", axis=1, tiled=True)
    total = lax.dot_general(
        acts, grads, (((0, 1), (0, 1)), ((), ())), preferred_element_type=jnp.float32
    )
    return total.astype(jnp.bfloat16)


def solution(mesh):
    in_specs = (P(("parts", "depth"), "row", "col"), P(("parts", "depth"), "col", "row"))
    out_specs = P(("parts", "col", "depth"), "row")
    return jax.shard_map(local, mesh=mesh, in_specs=in_specs, out_specs=out_specs, check_vma=False)
```

```python
import functools

import jax
import jax.numpy as jnp
from jax import lax
from jax.experimental import pallas as pl
from jax.experimental.pallas import tpu as pltpu
from jax.sharding import PartitionSpec as P

MESH = pl.DeviceIdType.MESH
MIB = 1024 * 1024
ROWS, COLS, DEPTH = 8, 1, 4
NZ = 4
TILE = 256
SHIFTED = (1, 3)
PARTS = 2


def product_tile(acts, grads, slot, tile):
    cols = pl.ds(pl.multiple_of(tile * TILE, TILE), TILE)
    lhs = acts[slot, :, :, cols]
    lhs = lhs.reshape(lhs.shape[0] * lhs.shape[1], TILE)
    return lax.dot_general(
        lhs, grads[slot], (((0,), (0,)), ((), ())), preferred_element_type=jnp.float32
    )


def gather_kernel(x_hbm, g_hbm, total, acts, grads, local_sem, recv_a, up_sem, down_sem, y_sem, ex_sem, recv_g, send_g):
    row, me = lax.axis_index("row"), lax.axis_index("depth")
    z, y = row // 2, row % 2
    width = acts.shape[3]
    tokens = grads.shape[1]
    one = me + 1 - 2 * (me % 2)
    peers = (me, one, (me + 2) % 4, (one + 2) % 4)
    near = z + 1 - 2 * (z % 2)
    here = 2 * z + y
    across = 2 * z + 1 - y

    def block(k):
        return x_hbm.at[0, :, pl.ds(pl.multiple_of(peers[k] * width, width), width)]

    own_x = pltpu.make_async_copy(block(0), acts.at[0, here], local_sem.at[0])
    own_g = pltpu.make_async_copy(g_hbm.at[0], grads.at[0], local_sem.at[1])
    own_x.start()
    own_g.start()

    barrier = pltpu.get_barrier_semaphore()
    for k in (1, 2, 3):
        pl.semaphore_signal(barrier, inc=1, device_id={"depth": peers[k]}, device_id_type=MESH)
    pl.semaphore_signal(barrier, inc=1, device_id={"row": across}, device_id_type=MESH)

    @pl.when(z > 0)
    def _():
        pl.semaphore_signal(barrier, inc=1, device_id={"row": here - 2}, device_id_type=MESH)

    @pl.when(z < NZ - 1)
    def _():
        pl.semaphore_signal(barrier, inc=1, device_id={"row": here + 2}, device_id_type=MESH)

    pl.semaphore_wait(barrier, 5 + ((z + 1) // 2) % 2)

    def exchange(k):
        return pltpu.make_async_remote_copy(
            block(k), acts.at[k, here], ex_sem.at[k - 1], recv_a.at[k, here],
            device_id={"depth": peers[k]}, device_id_type=MESH,
        )

    def send(j, r, sems, target):
        return pltpu.make_async_remote_copy(
            acts.at[j, r], acts.at[j, r], sems.at[j, r], recv_a.at[j, r],
            device_id={"row": target}, device_id_type=MESH,
        )

    def arrived(j, r):
        send(j, r, y_sem, across).wait_recv()

    part = tokens // PARTS

    def grads_to(k, p):
        rows = pl.ds(p * part, part)
        return pltpu.make_async_remote_copy(
            g_hbm.at[0, rows], grads.at[k, rows], send_g.at[k - 1, p], recv_g.at[k - 1, p],
            device_id={"depth": peers[k]}, device_id_type=MESH,
        )

    def grads_on(p):
        rows = pl.ds(p * part, part)
        return pltpu.make_async_remote_copy(
            grads.at[2, rows], grads.at[3, rows], send_g.at[2, p], recv_g.at[2, p],
            device_id={"depth": peers[1]}, device_id_type=MESH,
        )

    def forward_g(p):
        grads_to(2, p).wait_recv()
        grads_on(p).start()

    def moves(j, origin, go_up, go_down, wait):
        r = 2 * origin + y

        def steps():
            if wait:
                arrived(j, r)
            for going, sems, edge, target in (
                (go_up, up_sem, z < NZ - 1, here + 2),
                (go_down, down_sem, z > 0, here - 2),
            ):
                if going:
                    @pl.when(edge)
                    def _():
                        send(j, r, sems, target).start()
            if j in SHIFTED:
                @pl.when(origin != near)
                def _():
                    send(j, r, y_sem, across).start()
            else:
                send(j, r, y_sem, across).start()

        return steps

    def own(j):
        moves(j, z, True, True, j > 0)()

    def reach(j, dist):
        pl.when(z >= dist)(moves(j, z - dist, True, False, True))
        pl.when(z + dist < NZ)(moves(j, z + dist, False, True, True))

    def turn(j):
        arrived(j, across)
        even = z % 2 == 0

        @pl.when(even)
        def _():
            send(j, across, up_sem, here + 2).start()

        @pl.when(jnp.logical_not(even))
        def _():
            send(j, across, down_sem, here - 2).start()

    def finish(j):
        for origin in range(NZ):
            r = 2 * origin + 1 - y
            if j in SHIFTED:
                @pl.when(z != origin)
                def _():
                    arrived(j, r)
            else:
                arrived(j, r)

    def product(j, first, last):
        @pl.loop(first, last)
        def _(tile):
            rows = pl.ds(pl.multiple_of(tile * TILE, TILE), TILE)
            value = product_tile(acts, grads, j, tile)
            if j == 0:
                total[rows, :] = value
            else:
                total[rows, :] = total[rows, :] + value

    tiles = width // TILE

    own_x.wait()
    own(0)
    exchange(1).start()
    exchange(2).start()
    exchange(3).start()
    for p in range(PARTS):
        grads_to(2, p).start()
    for p in range(PARTS):
        grads_to(1, p).start()
    own(1)
    own_g.wait()
    reach(0, 1)
    own(2)
    reach(1, 1)
    turn(1)
    reach(0, 2)
    own(3)
    reach(2, 1)
    reach(1, 2)
    reach(0, 3)
    forward_g(0)
    turn(3)
    reach(3, 1)
    finish(0)
    product(0, 0, tiles // 4)
    reach(2, 2)
    product(0, tiles // 4, tiles // 2)
    reach(1, 3)
    product(0, tiles // 2, tiles)
    forward_g(1)
    reach(3, 2)
    for p in range(PARTS):
        grads_to(1, p).wait_recv()
    finish(1)
    product(1, 0, tiles // 2)
    reach(2, 3)
    product(1, tiles // 2, tiles)
    reach(3, 3)
    finish(2)
    product(2, 0, tiles)
    finish(3)
    for p in range(PARTS):
        grads_on(p).wait_recv()

    for k in (1, 2, 3):
        exchange(k).wait_send()
    for p in range(PARTS):
        grads_to(1, p).wait_send()
        grads_to(2, p).wait_send()
        grads_on(p).wait_send()
    for j in range(DEPTH):
        for origin in range(NZ):
            mine = 2 * origin + y

            @pl.when(jnp.logical_and(origin <= z, z < NZ - 1))
            def _():
                send(j, mine, up_sem, here + 2).wait_send()

            @pl.when(jnp.logical_and(origin >= z, z > 0))
            def _():
                send(j, mine, down_sem, here - 2).wait_send()

            if j in SHIFTED:
                @pl.when(near != origin)
                def _():
                    send(j, mine, y_sem, across).wait_send()
            else:
                send(j, mine, y_sem, across).wait_send()
        if j in SHIFTED:
            @pl.when(z % 2 == 0)
            def _():
                send(j, across, up_sem, here + 2).wait_send()

            @pl.when(z % 2 == 1)
            def _():
                send(j, across, down_sem, here - 2).wait_send()


def last_kernel(total, acts, grads, out_hbm, held, sems):
    tiles = total.shape[0] // TILE

    def copy(tile, slot):
        rows = pl.ds(pl.multiple_of(tile * TILE, TILE), TILE)
        return pltpu.make_async_copy(held.at[slot], out_hbm.at[rows], sems.at[slot])

    @pl.loop(0, tiles)
    def _(tile):
        slot = tile % 2
        rows = pl.ds(pl.multiple_of(tile * TILE, TILE), TILE)
        value = total[rows, :] + product_tile(acts, grads, DEPTH - 1, tile)

        @pl.when(tile >= 2)
        def _():
            copy(tile - 2, slot).wait()

        held[slot] = value.astype(held.dtype)
        copy(tile, slot).start()

    for tile in (tiles - 2, tiles - 1):
        copy(tile, tile % 2).wait()


def by_kernels(activations, hidden_grads):
    tokens, features = activations.shape[1], activations.shape[2] // DEPTH
    all_tokens, hidden = hidden_grads.shape[1], hidden_grads.shape[2]
    dtype = activations.dtype
    flops = 2 * features * hidden * all_tokens
    total, acts, grads = pl.pallas_call(
        gather_kernel,
        out_shape=(
            pltpu.VMEM((features, hidden), jnp.float32),
            pltpu.VMEM((DEPTH, ROWS, tokens, features), dtype),
            pltpu.VMEM((DEPTH, all_tokens, hidden), dtype),
        ),
        in_specs=[pl.BlockSpec(memory_space=pl.ANY)] * 2,
        out_specs=(pl.BlockSpec(memory_space=pltpu.VMEM),) * 3,
        scratch_shapes=[
            pltpu.SemaphoreType.DMA((2,)),
            pltpu.SemaphoreType.DMA((DEPTH, ROWS)),
            pltpu.SemaphoreType.DMA((DEPTH, ROWS)),
            pltpu.SemaphoreType.DMA((DEPTH, ROWS)),
            pltpu.SemaphoreType.DMA((DEPTH, ROWS)),
            pltpu.SemaphoreType.DMA((3,)),
            pltpu.SemaphoreType.DMA((3, PARTS)),
            pltpu.SemaphoreType.DMA((3, PARTS)),
        ],
        compiler_params=pltpu.CompilerParams(
            collective_id=0, has_side_effects=True, vmem_limit_bytes=12 * MIB
        ),
        cost_estimate=pl.CostEstimate(flops=3 * flops, bytes_accessed=10 * MIB, transcendentals=0),
        name="gather",
    )(activations, hidden_grads)
    return pl.pallas_call(
        last_kernel,
        out_shape=jax.ShapeDtypeStruct((features, hidden), dtype),
        in_specs=[pl.BlockSpec(memory_space=pltpu.VMEM)] * 3,
        out_specs=pl.BlockSpec(memory_space=pl.ANY),
        scratch_shapes=[pltpu.VMEM((2, TILE, hidden), dtype), pltpu.SemaphoreType.DMA((2,))],
        compiler_params=pltpu.CompilerParams(vmem_limit_bytes=12 * MIB),
        cost_estimate=pl.CostEstimate(flops=flops, bytes_accessed=8 * MIB, transcendentals=0),
        name="last",
    )(total, acts, grads)


def by_ops(activations, hidden_grads):
    swapped = lax.all_to_all(activations, "depth", split_axis=2, concat_axis=0, tiled=True)
    acts = lax.all_gather(swapped, "row", axis=1, tiled=True)
    grads = lax.all_gather(hidden_grads, "depth", axis=0, tiled=True)
    grads = lax.all_gather(grads, "col", axis=1, tiled=True)
    total = lax.dot_general(
        acts, grads, (((0, 1), (0, 1)), ((), ())), preferred_element_type=jnp.float32
    )
    return total.astype(jnp.bfloat16)


def solution(mesh):
    in_specs = (P(("parts", "depth"), "row", "col"), P(("parts", "depth"), "col", "row"))
    out_specs = P(("parts", "col", "depth"), "row")
    sizes = (mesh.shape["row"], mesh.shape["col"], mesh.shape["depth"])
    local = by_kernels if sizes == (ROWS, COLS, DEPTH) else by_ops
    return jax.shard_map(local, mesh=mesh, in_specs=in_specs, out_specs=out_specs, check_vma=False)
```

```python
import functools

import jax
import jax.numpy as jnp
from jax import lax
from jax.experimental import pallas as pl
from jax.experimental.pallas import tpu as pltpu
from jax.sharding import PartitionSpec as P

MESH = pl.DeviceIdType.MESH
MIB = 1024 * 1024
ROWS, COLS, DEPTH = 8, 1, 4
NZ = 4
LAST_TILE, LAST_COPIES = 512, 4
TILE = 256
SHIFTED = (1, 3)
PARTS = 2


def columns(tile):
    return pl.ds(pl.multiple_of(tile * TILE, TILE), TILE)


def product_tile(acts, grads, slot, tile):
    rows, tokens, width = acts.shape[1:]
    return lax.dot_general(
        acts[slot].reshape(rows * tokens, width),
        grads[slot, :, columns(tile)],
        (((0,), (0,)), ((), ())),
        preferred_element_type=jnp.float32,
    )


def gather_kernel(x_hbm, g_hbm, total, acts, grads, local_sem, recv_a, up_sem, down_sem, y_sem, ex_sem, recv_g, send_g):
    row, me = lax.axis_index("row"), lax.axis_index("depth")
    z, y = row // 2, row % 2
    width = acts.shape[3]
    tokens = grads.shape[1]
    one = me + 1 - 2 * (me % 2)
    peers = (me, one, (me + 2) % 4, (one + 2) % 4)
    near = z + 1 - 2 * (z % 2)
    here = 2 * z + y
    across = 2 * z + 1 - y

    def block(k):
        return x_hbm.at[0, :, pl.ds(pl.multiple_of(peers[k] * width, width), width)]

    own_x = pltpu.make_async_copy(block(0), acts.at[0, here], local_sem.at[0])
    own_g = pltpu.make_async_copy(g_hbm.at[0], grads.at[0], local_sem.at[1])
    own_x.start()
    own_g.start()

    barrier = pltpu.get_barrier_semaphore()
    for k in (1, 2, 3):
        pl.semaphore_signal(barrier, inc=1, device_id={"depth": peers[k]}, device_id_type=MESH)
    pl.semaphore_signal(barrier, inc=1, device_id={"row": across}, device_id_type=MESH)

    @pl.when(z > 0)
    def _():
        pl.semaphore_signal(barrier, inc=1, device_id={"row": here - 2}, device_id_type=MESH)

    @pl.when(z < NZ - 1)
    def _():
        pl.semaphore_signal(barrier, inc=1, device_id={"row": here + 2}, device_id_type=MESH)

    pl.semaphore_wait(barrier, 5 + ((z + 1) // 2) % 2)

    def exchange(k):
        return pltpu.make_async_remote_copy(
            block(k), acts.at[k, here], ex_sem.at[k - 1], recv_a.at[k, here],
            device_id={"depth": peers[k]}, device_id_type=MESH,
        )

    def send(j, r, sems, target):
        return pltpu.make_async_remote_copy(
            acts.at[j, r], acts.at[j, r], sems.at[j, r], recv_a.at[j, r],
            device_id={"row": target}, device_id_type=MESH,
        )

    def arrived(j, r):
        send(j, r, y_sem, across).wait_recv()

    part = tokens // PARTS

    def grads_to(k, p):
        rows = pl.ds(p * part, part)
        return pltpu.make_async_remote_copy(
            g_hbm.at[0, rows], grads.at[k, rows], send_g.at[k - 1, p], recv_g.at[k - 1, p],
            device_id={"depth": peers[k]}, device_id_type=MESH,
        )

    def grads_on(p):
        rows = pl.ds(p * part, part)
        return pltpu.make_async_remote_copy(
            grads.at[2, rows], grads.at[3, rows], send_g.at[2, p], recv_g.at[2, p],
            device_id={"depth": peers[1]}, device_id_type=MESH,
        )

    def forward_g(p):
        grads_to(2, p).wait_recv()
        grads_on(p).start()

    def moves(j, origin, go_up, go_down, wait):
        r = 2 * origin + y

        def steps():
            if wait:
                arrived(j, r)
            for going, sems, edge, target in (
                (go_up, up_sem, z < NZ - 1, here + 2),
                (go_down, down_sem, z > 0, here - 2),
            ):
                if going:
                    @pl.when(edge)
                    def _():
                        send(j, r, sems, target).start()
            if j in SHIFTED:
                @pl.when(origin != near)
                def _():
                    send(j, r, y_sem, across).start()
            else:
                send(j, r, y_sem, across).start()

        return steps

    def own(j):
        moves(j, z, True, True, j > 0)()

    def from_below(j, dist):
        pl.when(z >= dist)(moves(j, z - dist, True, False, True))

    def from_above(j, dist):
        pl.when(z + dist < NZ)(moves(j, z + dist, False, True, True))

    def turn(j):
        arrived(j, across)
        even = z % 2 == 0

        @pl.when(even)
        def _():
            send(j, across, up_sem, here + 2).start()

        @pl.when(jnp.logical_not(even))
        def _():
            send(j, across, down_sem, here - 2).start()

    def ready(j):
        for origin in range(NZ):
            r = 2 * origin + 1 - y
            if j in SHIFTED:
                @pl.when(z != origin)
                def _():
                    arrived(j, r)
            else:
                arrived(j, r)
        if j == 0:
            own_g.wait()
        for p in range(PARTS):
            if j == 1:
                grads_to(1, p).wait_recv()
            elif j == 3:
                grads_on(p).wait_recv()

    def product(j, first, last):
        @pl.loop(first, last)
        def _(tile):
            value = product_tile(acts, grads, j, tile)
            if j == 0:
                total[:, columns(tile)] = value
            else:
                total[:, columns(tile)] = total[:, columns(tile)] + value

    tiles = total.shape[1] // TILE

    own_x.wait()
    own(0)
    for k in (1, 2, 3):
        exchange(k).start()
    for p in range(PARTS):
        grads_to(2, p).start()
    for p in range(PARTS):
        grads_to(1, p).start()
    own(1)
    from_above(0, 1)
    own(2)
    from_below(0, 1)
    from_below(2, 1)
    from_above(0, 2)
    from_below(0, 2)
    from_below(0, 3)
    from_above(2, 1)
    own(3)
    from_below(2, 2)
    from_above(0, 3)
    from_below(1, 1)
    from_above(2, 2)
    from_below(2, 3)
    from_above(1, 1)
    from_above(2, 3)
    from_above(1, 2)
    from_below(1, 2)
    ready(0)
    product(0, 0 * tiles // 8, 1 * tiles // 8)
    turn(1)
    from_below(3, 1)
    product(0, 1 * tiles // 8, 2 * tiles // 8)
    from_above(3, 1)
    product(0, 2 * tiles // 8, 8 * tiles // 8)
    from_below(1, 3)
    from_above(1, 3)
    forward_g(0)
    forward_g(1)
    ready(2)
    product(2, 0 * tiles // 8, 4 * tiles // 8)
    from_below(3, 2)
    from_above(3, 2)
    product(2, 4 * tiles // 8, 6 * tiles // 8)
    turn(3)
    product(2, 6 * tiles // 8, 8 * tiles // 8)
    from_below(3, 3)
    from_above(3, 3)
    ready(1)
    product(1, 0 * tiles // 8, 8 * tiles // 8)
    ready(DEPTH - 1)

    for k in (1, 2, 3):
        exchange(k).wait_send()
    for p in range(PARTS):
        grads_to(1, p).wait_send()
        grads_to(2, p).wait_send()
        grads_on(p).wait_send()
    for j in range(DEPTH):
        for origin in range(NZ):
            mine = 2 * origin + y

            @pl.when(jnp.logical_and(origin <= z, z < NZ - 1))
            def _():
                send(j, mine, up_sem, here + 2).wait_send()

            @pl.when(jnp.logical_and(origin >= z, z > 0))
            def _():
                send(j, mine, down_sem, here - 2).wait_send()

            if j in SHIFTED:
                @pl.when(near != origin)
                def _():
                    send(j, mine, y_sem, across).wait_send()
            else:
                send(j, mine, y_sem, across).wait_send()
        if j in SHIFTED:
            @pl.when(z % 2 == 0)
            def _():
                send(j, across, up_sem, here + 2).wait_send()

            @pl.when(z % 2 == 1)
            def _():
                send(j, across, down_sem, here - 2).wait_send()


def last_kernel(total, acts, grads, out_hbm, held, sems):
    last = DEPTH - 1
    rows, tokens = acts.shape[1:3]
    tiles = total.shape[0] // LAST_TILE
    part = LAST_TILE // LAST_COPIES

    def copies(tile):
        for p in range(LAST_COPIES):
            some = pl.ds(pl.multiple_of(tile * LAST_TILE + p * part, part), part)
            yield pltpu.make_async_copy(held.at[some], out_hbm.at[some], sems.at[tile, p])

    @pl.loop(0, tiles)
    def _(tile):
        some = pl.ds(pl.multiple_of(tile * LAST_TILE, LAST_TILE), LAST_TILE)
        value = total[some, :] + lax.dot_general(
            acts[last, :, :, some].reshape(rows * tokens, LAST_TILE),
            grads[last],
            (((0,), (0,)), ((), ())),
            preferred_element_type=jnp.float32,
        )
        held[some, :] = value.astype(held.dtype)
        for copy in copies(tile):
            copy.start()

    @pl.loop(0, tiles)
    def _(tile):
        for copy in copies(tile):
            copy.wait()


def by_kernels(activations, hidden_grads):
    tokens, features = activations.shape[1], activations.shape[2] // DEPTH
    all_tokens, hidden = hidden_grads.shape[1], hidden_grads.shape[2]
    dtype = activations.dtype
    flops = 2 * features * hidden * all_tokens
    total, acts, grads = pl.pallas_call(
        gather_kernel,
        out_shape=(
            pltpu.VMEM((features, hidden), jnp.float32),
            pltpu.VMEM((DEPTH, ROWS, tokens, features), dtype),
            pltpu.VMEM((DEPTH, all_tokens, hidden), dtype),
        ),
        in_specs=[pl.BlockSpec(memory_space=pl.ANY)] * 2,
        out_specs=(pl.BlockSpec(memory_space=pltpu.VMEM),) * 3,
        scratch_shapes=[
            pltpu.SemaphoreType.DMA((2,)),
            pltpu.SemaphoreType.DMA((DEPTH, ROWS)),
            pltpu.SemaphoreType.DMA((DEPTH, ROWS)),
            pltpu.SemaphoreType.DMA((DEPTH, ROWS)),
            pltpu.SemaphoreType.DMA((DEPTH, ROWS)),
            pltpu.SemaphoreType.DMA((3,)),
            pltpu.SemaphoreType.DMA((3, PARTS)),
            pltpu.SemaphoreType.DMA((3, PARTS)),
        ],
        compiler_params=pltpu.CompilerParams(
            collective_id=0, has_side_effects=True, vmem_limit_bytes=12 * MIB
        ),
        cost_estimate=pl.CostEstimate(flops=3 * flops, bytes_accessed=10 * MIB, transcendentals=0),
        name="gather",
    )(
        pltpu.with_memory_space_constraint(activations, pltpu.HBM),
        pltpu.with_memory_space_constraint(hidden_grads, pltpu.HBM),
    )
    return pl.pallas_call(
        last_kernel,
        out_shape=jax.ShapeDtypeStruct((features, hidden), dtype),
        in_specs=[pl.BlockSpec(memory_space=pltpu.VMEM)] * 3,
        out_specs=pl.BlockSpec(memory_space=pl.ANY),
        scratch_shapes=[
            pltpu.VMEM((features, hidden), dtype),
            pltpu.SemaphoreType.DMA((features // LAST_TILE, LAST_COPIES)),
        ],
        compiler_params=pltpu.CompilerParams(vmem_limit_bytes=20 * MIB),
        cost_estimate=pl.CostEstimate(flops=flops, bytes_accessed=8 * MIB, transcendentals=0),
        name="last",
    )(total, acts, grads)


def by_ops(activations, hidden_grads):
    swapped = lax.all_to_all(activations, "depth", split_axis=2, concat_axis=0, tiled=True)
    acts = lax.all_gather(swapped, "row", axis=1, tiled=True)
    grads = lax.all_gather(hidden_grads, "depth", axis=0, tiled=True)
    grads = lax.all_gather(grads, "col", axis=1, tiled=True)
    total = lax.dot_general(
        acts, grads, (((0, 1), (0, 1)), ((), ())), preferred_element_type=jnp.float32
    )
    return total.astype(jnp.bfloat16)


def solution(mesh):
    in_specs = (P(("parts", "depth"), "row", "col"), P(("parts", "depth"), "col", "row"))
    out_specs = P(("parts", "col", "depth"), "row")
    sizes = (mesh.shape["row"], mesh.shape["col"], mesh.shape["depth"])
    local = by_kernels if sizes == (ROWS, COLS, DEPTH) else by_ops
    return jax.shard_map(local, mesh=mesh, in_specs=in_specs, out_specs=out_specs, check_vma=False)
```
